32 devices in a mesh: group: 2 (over x), cand: 16 (over z, y, core).
Axes of the slice: x: 2, y: 2, z: 4, core: 2. Of those that a mesh axis runs over, the one named last changes fastest.
Arguments:
- embeddings: bfloat16 [64, 1024, 768], P(('group', 'cand')), parts along dimension 0
- lengths: int32 [64], P(('group', 'cand')), parts along dimension 0, may hold values from 256 to 1024, as said below
Outputs:
- consensus: float32 [64, 1024], P(('group', 'cand')), parts along dimension 0
The draws below stay inside these ranges and needn't reach their ends.
There are 2 independent parts, one for each index of `group`. The reference program is written for one: setup_inputs(seed, part) draws one part's arguments, and reference() takes and returns one part's arrays. A program takes and returns all parts, laid end to end along the dimension named above; each array names one. Nothing has to cross between parts.
Inputs may be any that keep to these rules, and one draw needn't show every extreme that they name: `lengths`: at least one answer of every prompt has exactly 1024 tokens; every answer has 256 tokens or more.
All inputs are finite; a program needn't handle non-finite values.
Results may differ from the reference program's by a relative error of at most 0.0005.
Values may be sent and summed in bfloat16 or wider, within the bound.
No kernel may reach another device: no remote copies, remote signals or barrier semaphores. Data moves between devices by JAX's collectives and lax.ppermute only.
A program may use at most 64 MiB of HBM per device.

```python
import jax
import jax.numpy as jnp
from jax import lax

A_DEV = 2
L = 1024
E = 768
ROUNDS = 2
CAND = 32
PARTNERS = 9
N_CAND = 16


def draw_embeddings(key, part):
    key_base = jax.random.fold_in(key, 11)
    base = jax.random.normal(key_base, (CAND, L, E), jnp.float32)
    return base.astype(jnp.bfloat16)


def draw_lengths(key, part):
    drawn = jax.random.randint(jax.random.fold_in(key, 21), (CAND,), L // 4, L + 1)
    where_full = jax.random.randint(jax.random.fold_in(key, 22), (), 0, CAND)
    return drawn.at[where_full].set(L).astype(jnp.int32)


def setup_inputs(seed: int = 0, part: int = 0) -> dict:
    streams_of = jax.random.split(jax.random.key(seed), 3)
    own_keys = jax.random.split(jax.random.fold_in(streams_of[2], part), 3)
    return {
        "embeddings": draw_embeddings(jax.random.fold_in(jax.random.fold_in(streams_of[2], part), 71), part),
        "lengths": draw_lengths(jax.random.fold_in(jax.random.fold_in(streams_of[2], part), 71), part),
    }


INV_TEMP = 256.0

def unit_rows(embeddings):
    values = embeddings.astype(jnp.float32)
    scale = lax.rsqrt(lax.optimization_barrier(jnp.sum(values * values, axis=-1, keepdims=True)) + 1e-06)
    return (values * scale).astype(jnp.bfloat16)

def soft_terms(left, left_valid, right, right_valid):
    scores = jnp.einsum('te,bse->bts', left.astype(jnp.float32), right.astype(jnp.float32)) * INV_TEMP
    row_scores = jnp.where(right_valid[:, None, :] > 0.5, scores, -1e+30)
    row_peak = lax.optimization_barrier(jnp.max(row_scores, axis=2, keepdims=True))
    row_terms = (row_peak[..., 0] + jnp.log(lax.optimization_barrier(jnp.sum(jnp.exp(row_scores - row_peak), axis=2)))) / INV_TEMP
    col_scores = jnp.where(left_valid[None, :, None] > 0.5, scores, -1e+30)
    col_peak = lax.optimization_barrier(jnp.max(col_scores, axis=1, keepdims=True))
    col_terms = (col_peak[:, 0, :] + jnp.log(lax.optimization_barrier(jnp.sum(jnp.exp(col_scores - col_peak), axis=1)))) / INV_TEMP
    return (row_terms, col_terms)

def reference(embeddings, lengths):
    unit = unit_rows(embeddings)
    valid = (jnp.arange(L, dtype=jnp.int32)[None, :] < lengths[:, None]).astype(jnp.float32)

    def visit(totals, index):
        block = index // A_DEV
        start = (block * A_DEV).astype(jnp.int32)
        mine = unit[index]
        mine_valid = valid[index]
        same = lax.dynamic_slice_in_dim(unit, start, A_DEV, 0)
        same_valid = lax.dynamic_slice_in_dim(valid, start, A_DEV, 0)
        row_terms, unused = soft_terms(mine, mine_valid, same, same_valid)
        weight = (jnp.arange(A_DEV, dtype=jnp.int32) + start != index).astype(jnp.float32)
        own_sum = lax.optimization_barrier(jnp.sum(row_terms * weight[:, None], axis=0))
        for offset in range(1, ROUNDS + 1):
            other = ((block - offset) % N_CAND * A_DEV).astype(jnp.int32)
            theirs = lax.dynamic_slice_in_dim(unit, other, A_DEV, 0)
            their_valid = lax.dynamic_slice_in_dim(valid, other, A_DEV, 0)
            row_terms, col_terms = soft_terms(mine, mine_valid, theirs, their_valid)
            own_sum = own_sum + lax.optimization_barrier(jnp.sum(row_terms, axis=0))
            current = lax.dynamic_slice_in_dim(totals, other, A_DEV, 0)
            totals = lax.dynamic_update_slice_in_dim(totals, current + col_terms, other, 0)
        totals = totals.at[index].add(own_sum)
        return (totals, None)
    totals, unused = lax.scan(visit, jnp.zeros((CAND, L), jnp.float32), jnp.arange(CAND, dtype=jnp.int32))
    return totals * valid / PARTNERS
```

```python
import functools

import jax
import jax.numpy as jnp
from jax import lax
from jax.experimental import pallas as pl
from jax.experimental.pallas import tpu as pltpu
from jax.sharding import PartitionSpec as P

SCALE = 256.0 * 1.4426950408889634
LOWEST = -1e30
LANES = 128
ROW_TILE = 1024
COL_TILE = 512
SUM_TILE = 256
SUM_STEP = 64


def unit_rows(embeddings):
    values = embeddings.astype(jnp.float32)
    scale = lax.rsqrt(jnp.sum(values * values, axis=-1, keepdims=True) + 1e-06)
    return (values * scale).astype(jnp.bfloat16)


def unit_kernel(values_ref, unit_ref):
    unit_ref[...] = unit_rows(values_ref[...])


def make_unit(embeddings):
    answers, length, width = embeddings.shape
    rows = answers * length
    tile = min(512, rows)
    flat = pl.pallas_call(
        unit_kernel,
        grid=(rows // tile,),
        in_specs=[pl.BlockSpec((tile, width), lambda i: (i, 0))],
        out_specs=pl.BlockSpec((tile, width), lambda i: (i, 0)),
        out_shape=jax.ShapeDtypeStruct((rows, width), jnp.bfloat16),
    )(embeddings.reshape(rows, width))
    return flat.reshape(embeddings.shape)


def pair_kernel(meta, left_ref, right_ref, row_ref, col_ref, unit, scores, peak, total, *, raw):
    pair = pl.program_id(0)
    left_rows = left_ref.shape[1]
    right_rows = right_ref.shape[1]
    left_len = meta[2, pair]
    right_len = meta[3, pair]
    row_tile = min(ROW_TILE, left_rows)
    col_tile = min(COL_TILE, right_rows)
    sum_rows = min(SUM_TILE, left_rows)
    sum_cols = min(SUM_TILE, right_rows)

    if raw:

        @pl.when(pair == 0)
        def _():
            for start in range(0, left_rows, LANES):
                unit[start : start + LANES, :] = unit_rows(left_ref[0, start : start + LANES, :])

    row_ref[...] = jnp.zeros_like(row_ref)
    col_ref[...] = jnp.zeros_like(col_ref)

    def at(index, size):
        return pl.ds(pl.multiple_of(index * size, size), size)

    def steps(count, size):
        return lax.div(count + size - 1, size)

    @pl.when((left_len > 0) & (right_len > 0))
    def _():
        peak[...] = jnp.full_like(peak, LOWEST)
        total[...] = jnp.zeros_like(total)

        def score_cols(j, carry):
            cols = at(j, col_tile)
            right = right_ref[0, cols, :]
            col_at = lax.broadcasted_iota(jnp.int32, (1, col_tile), 1) + j * col_tile
            col_bias = jnp.where(col_at < right_len, 0.0, LOWEST)

            def score_rows(i, col_peak):
                rows = at(i, row_tile)
                left = unit[rows, :] if raw else left_ref[0, rows, :]
                tile = lax.dot_general(
                    left, right, (((1,), (1,)), ((), ())), preferred_element_type=jnp.float32
                )
                row_at = lax.broadcasted_iota(jnp.int32, (row_tile, 1), 0) + i * row_tile
                row_bias = jnp.where(row_at < left_len, 0.0, LOWEST)
                tile = (tile * SCALE + col_bias) + row_bias
                scores[rows, cols] = tile
                row_peak = peak[rows, :]
                for k in range(0, col_tile, LANES):
                    row_peak = jnp.maximum(row_peak, tile[:, k : k + LANES])
                peak[rows, :] = row_peak
                folded = jnp.max(tile.reshape(row_tile // 8, 8, col_tile), axis=0)
                return jnp.maximum(col_peak, folded)

            col_peak = lax.fori_loop(
                0, steps(left_len, row_tile), score_rows, jnp.full((8, col_tile), LOWEST, jnp.float32)
            )
            col_ref[0, :, cols] = jnp.max(col_peak, axis=0, keepdims=True)
            return carry

        lax.fori_loop(0, steps(right_len, col_tile), score_cols, 0)

        def sum_cols_of(j, carry):
            cols = at(j, sum_cols)
            col_peak = col_ref[0, :, cols]

            def sum_rows_of(i, col_sum):
                for step in range(0, sum_rows, SUM_STEP):
                    rows = pl.ds(pl.multiple_of(i * sum_rows, sum_rows) + step, SUM_STEP)
                    tile = scores[rows, cols]
                    row_peak = peak[rows, :]
                    row_sum = total[rows, :]
                    for k in range(0, sum_cols, LANES):
                        row_sum = row_sum + jnp.exp2(tile[:, k : k + LANES] - row_peak)
                    total[rows, :] = row_sum
                    terms = jnp.exp2(tile - col_peak)
                    col_sum = col_sum + jnp.sum(terms.reshape(SUM_STEP // 8, 8, sum_cols), axis=0)
                return col_sum

            col_sum = lax.fori_loop(
                0, steps(left_len, sum_rows), sum_rows_of, jnp.zeros((8, sum_cols), jnp.float32)
            )
            col_sum = jnp.sum(col_sum, axis=0, keepdims=True)
            col_ref[0, :, cols] = (col_peak + jnp.log2(col_sum)) * (1.0 / SCALE)
            return carry

        lax.fori_loop(0, steps(right_len, sum_cols), sum_cols_of, 0)

        def finish_rows(i, carry):
            rows = at(i, sum_rows)
            lane_peak = jnp.transpose(peak[rows, :])
            lane_sum = jnp.transpose(total[rows, :])
            row_peak = jnp.max(lane_peak, axis=0, keepdims=True)
            row_sum = jnp.sum(lane_sum * jnp.exp2(lane_peak - row_peak), axis=0, keepdims=True)
            row_ref[0, :, rows] = (row_peak + jnp.log2(row_sum)) * (1.0 / SCALE)
            return carry

        lax.fori_loop(0, steps(left_len, sum_rows), finish_rows, 0)


def match_pairs(meta, left, right, raw):
    pairs = meta.shape[1]
    left_rows, width = left.shape[1:]
    right_rows = right.shape[1]
    rows, cols = pl.pallas_call(
        functools.partial(pair_kernel, raw=raw),
        grid_spec=pltpu.PrefetchScalarGridSpec(
            num_scalar_prefetch=1,
            grid=(pairs,),
            in_specs=[
                pl.BlockSpec((1, left_rows, width), lambda p, m: (m[0, p], 0, 0)),
                pl.BlockSpec((1, right_rows, width), lambda p, m: (m[1, p], 0, 0)),
            ],
            out_specs=[
                pl.BlockSpec((1, 1, left_rows), lambda p, m: (p, 0, 0)),
                pl.BlockSpec((1, 1, right_rows), lambda p, m: (p, 0, 0)),
            ],
            scratch_shapes=[
                pltpu.VMEM((left_rows if raw else 16, width), jnp.bfloat16),
                pltpu.VMEM((left_rows, right_rows), jnp.float32),
                pltpu.VMEM((left_rows, LANES), jnp.float32),
                pltpu.VMEM((left_rows, LANES), jnp.float32),
            ],
        ),
        out_shape=[
            jax.ShapeDtypeStruct((pairs, 1, left_rows), jnp.float32),
            jax.ShapeDtypeStruct((pairs, 1, right_rows), jnp.float32),
        ],
        compiler_params=pltpu.CompilerParams(vmem_limit_bytes=32 << 20),
        cost_estimate=pl.CostEstimate(
            flops=2 * pairs * left_rows * right_rows * width,
            bytes_accessed=2 * (pairs + 1) * right_rows * width,
            transcendentals=2 * pairs * left_rows * right_rows,
        ),
    )(meta, left, right)
    return rows[:, 0], cols[:, 0]


def after(value, *earlier):
    return lax.optimization_barrier((value, *earlier))[0]


def shards(embeddings, lengths):
    answers, length, _ = embeddings.shape
    count = lax.axis_size("cand")
    here = lax.axis_index("cand")
    is_even = here % 2 == 0

    first_to = [(i, (i - 2 if i % 2 == 0 else i + 2) % count) for i in range(count)]
    second_to = [(i, (i - 1 if i % 2 == 0 else i + 1) % count) for i in range(count)]
    mate_to = [(i, i ^ 1) for i in range(count)]

    def move(value, pairs):
        return lax.ppermute(value, "cand", pairs)

    def back(value, pairs):
        return lax.ppermute(value, "cand", [(b, a) for a, b in pairs])

    first = move(embeddings[0:1], first_to)
    unit = make_unit(embeddings)
    mate_unit = move(unit, mate_to)

    table = lax.all_gather(lengths, "cand", axis=0)

    def lengths_of(offset):
        return lax.dynamic_index_in_dim(table, (here + offset) % count, 0, keepdims=False)

    near = jnp.concatenate([lengths, jnp.where(is_even, lengths_of(1), lengths_of(-1))])
    own_only = jnp.arange(2 * answers, dtype=jnp.int32) < answers
    first_len = jnp.where(is_even, lengths_of(2)[0], lengths_of(-2)[0])
    second_len = jnp.where(is_even, lengths_of(-1)[1], lengths_of(1)[1])
    first_near = jnp.where(is_even | own_only, near, 0)
    second_near = jnp.where(is_even & own_only, 0, near)

    def meta_of(left, right, left_len, right_len):
        return jnp.stack([left, right, jnp.broadcast_to(left_len, right.shape), right_len]).astype(jnp.int32)

    residents = jnp.concatenate([unit, mate_unit])
    inner_left = jnp.where(is_even, jnp.array([0, 0, 0]), jnp.array([0, 3, 3]))
    inner_right = jnp.where(is_even, jnp.array([1, 2, 3]), jnp.array([1, 0, 1]))
    inner_meta = meta_of(inner_left, inner_right, near[inner_left], near[inner_right])
    rows, cols = match_pairs(inner_meta, residents, residents, False)
    zero = jnp.zeros_like(rows[0])
    totals = jnp.where(
        is_even,
        jnp.stack([rows[0] + rows[1] + rows[2], cols[0], cols[1], cols[2]]),
        jnp.stack([rows[0] + cols[1], cols[0] + cols[2], zero, rows[1] + rows[2]]),
    )

    second = move(after(embeddings[1:2], rows), second_to)
    every = jnp.arange(2 * answers)
    nothing = jnp.zeros_like(every)
    rows, cols = match_pairs(meta_of(nothing, every, first_len, first_near), first, residents, True)
    totals = totals + cols
    first_back = back(jnp.sum(rows, axis=0), first_to)
    rows, cols = match_pairs(meta_of(nothing, every, second_len, second_near), second, residents, True)
    totals = totals + cols
    second_back = back(jnp.sum(rows, axis=0), second_to)
    mate_back = move(totals[answers:], mate_to)

    consensus = totals[:answers] + mate_back + jnp.stack([first_back, second_back])
    inside = lax.broadcasted_iota(jnp.int32, (answers, length), 1) < lengths[:, None]
    return jnp.where(inside, consensus / (answers - 1 + 4 * answers), 0.0)


def solution(mesh):
    return jax.shard_map(
        shards,
        mesh=mesh,
        in_specs=(P(("group", "cand"), None, None), P(("group", "cand"))),
        out_specs=P(("group", "cand"), None),
        check_vma=False,
    )
```

```python
import functools

import jax
import jax.numpy as jnp
from jax import lax
from jax.experimental import pallas as pl
from jax.experimental.pallas import tpu as pltpu
from jax.sharding import PartitionSpec as P

SCALE = 256.0 * 1.4426950408889634
LOWEST = -1e30
LANES = 128
TAG_ROWS = 16
TAG_BASE = 64
ROW_TILE = 1024
COL_TILE = 512
SUM_TILE = 256
SUM_STEP = 64


def unit_rows(embeddings):
    values = embeddings.astype(jnp.float32)
    scale = lax.rsqrt(jnp.sum(values * values, axis=-1, keepdims=True) + 1e-06)
    return (values * scale).astype(jnp.bfloat16)


def tag_of(length, shape):
    top = lax.broadcasted_iota(jnp.int32, shape, len(shape) - 2) < TAG_ROWS // 2
    return jnp.where(top, length // TAG_BASE, length % TAG_BASE).astype(jnp.bfloat16)


def length_of(tag):
    values = tag.astype(jnp.float32)
    top = lax.broadcasted_iota(jnp.int32, values.shape, 0) < TAG_ROWS // 2
    high = jnp.max(jnp.where(top, values, 0.0))
    low = jnp.max(jnp.where(top, 0.0, values))
    return (high * TAG_BASE + low).astype(jnp.int32)


def packet_of(answer, length):
    return jnp.concatenate([answer, tag_of(length, (TAG_ROWS, answer.shape[1]))])[None]


def unit_kernel(lengths, values_ref, unit_ref):
    rows = values_ref.shape[1]
    for start in range(0, rows, LANES):
        unit_ref[0, start : start + LANES, :] = unit_rows(values_ref[0, start : start + LANES, :])
    unit_ref[0, rows:, :] = tag_of(lengths[pl.program_id(0)], (TAG_ROWS, values_ref.shape[2]))


def make_unit(embeddings, lengths):
    answers, length, width = embeddings.shape
    return pl.pallas_call(
        unit_kernel,
        grid_spec=pltpu.PrefetchScalarGridSpec(
            num_scalar_prefetch=1,
            grid=(answers,),
            in_specs=[pl.BlockSpec((1, length, width), lambda i, m: (i, 0, 0))],
            out_specs=pl.BlockSpec((1, length + TAG_ROWS, width), lambda i, m: (i, 0, 0)),
        ),
        out_shape=jax.ShapeDtypeStruct((answers, length + TAG_ROWS, width), jnp.bfloat16),
    )(lengths, embeddings)


def pair_kernel(meta, left_ref, right_ref, row_ref, col_ref, unit, scores, peak, total, *, raw):
    pair = pl.program_id(0)
    left_rows = left_ref.shape[1] - TAG_ROWS
    right_rows = right_ref.shape[1] - TAG_ROWS
    left_len = length_of(left_ref[0, left_rows:, :])
    right_len = length_of(right_ref[0, right_rows:, :])
    row_tile = min(ROW_TILE, left_rows)
    col_tile = min(COL_TILE, right_rows)
    sum_rows = min(SUM_TILE, left_rows)
    sum_cols = min(SUM_TILE, right_rows)

    if raw:

        @pl.when(pair == 0)
        def _():
            for start in range(0, left_rows, LANES):
                unit[start : start + LANES, :] = unit_rows(left_ref[0, start : start + LANES, :])

    row_ref[...] = jnp.zeros_like(row_ref)
    col_ref[...] = jnp.zeros_like(col_ref)

    def at(index, size):
        return pl.ds(pl.multiple_of(index * size, size), size)

    def steps(count, size):
        return lax.div(count + size - 1, size)

    @pl.when(meta[2, pair] > 0)
    def _():
        peak[...] = jnp.full_like(peak, LOWEST)
        total[...] = jnp.zeros_like(total)

        def score_cols(j, carry):
            cols = at(j, col_tile)
            right = right_ref[0, cols, :]
            col_at = lax.broadcasted_iota(jnp.int32, (1, col_tile), 1) + j * col_tile
            col_bias = jnp.where(col_at < right_len, 0.0, LOWEST)

            def score_rows(i, col_peak):
                rows = at(i, row_tile)
                left = unit[rows, :] if raw else left_ref[0, rows, :]
                tile = lax.dot_general(
                    left, right, (((1,), (1,)), ((), ())), preferred_element_type=jnp.float32
                )
                row_at = lax.broadcasted_iota(jnp.int32, (row_tile, 1), 0) + i * row_tile
                row_bias = jnp.where(row_at < left_len, 0.0, LOWEST)
                tile = (tile * SCALE + col_bias) + row_bias
                scores[rows, cols] = tile
                row_peak = peak[rows, :]
                for k in range(0, col_tile, LANES):
                    row_peak = jnp.maximum(row_peak, tile[:, k : k + LANES])
                peak[rows, :] = row_peak
                folded = jnp.max(tile.reshape(row_tile // 8, 8, col_tile), axis=0)
                return jnp.maximum(col_peak, folded)

            col_peak = lax.fori_loop(
                0, steps(left_len, row_tile), score_rows, jnp.full((8, col_tile), LOWEST, jnp.float32)
            )
            col_ref[0, :, cols] = jnp.max(col_peak, axis=0, keepdims=True)
            return carry

        lax.fori_loop(0, steps(right_len, col_tile), score_cols, 0)

        def sum_cols_of(j, carry):
            cols = at(j, sum_cols)
            col_peak = col_ref[0, :, cols]

            def sum_rows_of(i, col_sum):
                for step in range(0, sum_rows, SUM_STEP):
                    rows = pl.ds(pl.multiple_of(i * sum_rows, sum_rows) + step, SUM_STEP)
                    tile = scores[rows, cols]
                    row_peak = peak[rows, :]
                    row_sum = total[rows, :]
                    for k in range(0, sum_cols, LANES):
                        row_sum = row_sum + jnp.exp2(tile[:, k : k + LANES] - row_peak)
                    total[rows, :] = row_sum
                    terms = jnp.exp2(tile - col_peak)
                    col_sum = col_sum + jnp.sum(terms.reshape(SUM_STEP // 8, 8, sum_cols), axis=0)
                return col_sum

            col_sum = lax.fori_loop(
                0, steps(left_len, sum_rows), sum_rows_of, jnp.zeros((8, sum_cols), jnp.float32)
            )
            col_sum = jnp.sum(col_sum, axis=0, keepdims=True)
            col_ref[0, :, cols] = (col_peak + jnp.log2(col_sum)) * (1.0 / SCALE)
            return carry

        lax.fori_loop(0, steps(right_len, sum_cols), sum_cols_of, 0)

        def finish_rows(i, carry):
            rows = at(i, sum_rows)
            lane_peak = jnp.transpose(peak[rows, :])
            lane_sum = jnp.transpose(total[rows, :])
            row_peak = jnp.max(lane_peak, axis=0, keepdims=True)
            row_sum = jnp.sum(lane_sum * jnp.exp2(lane_peak - row_peak), axis=0, keepdims=True)
            row_ref[0, :, rows] = (row_peak + jnp.log2(row_sum)) * (1.0 / SCALE)
            return carry

        lax.fori_loop(0, steps(left_len, sum_rows), finish_rows, 0)


def match_pairs(meta, left, right, raw):
    pairs = meta.shape[1]
    width = left.shape[2]
    left_rows = left.shape[1] - TAG_ROWS
    right_rows = right.shape[1] - TAG_ROWS
    rows, cols = pl.pallas_call(
        functools.partial(pair_kernel, raw=raw),
        grid_spec=pltpu.PrefetchScalarGridSpec(
            num_scalar_prefetch=1,
            grid=(pairs,),
            in_specs=[
                pl.BlockSpec((1,) + left.shape[1:], lambda p, m: (m[0, p], 0, 0)),
                pl.BlockSpec((1,) + right.shape[1:], lambda p, m: (m[1, p], 0, 0)),
            ],
            out_specs=[
                pl.BlockSpec((1, 1, left_rows), lambda p, m: (p, 0, 0)),
                pl.BlockSpec((1, 1, right_rows), lambda p, m: (p, 0, 0)),
            ],
            scratch_shapes=[
                pltpu.VMEM((left_rows if raw else 16, width), jnp.bfloat16),
                pltpu.VMEM((left_rows, right_rows), jnp.float32),
                pltpu.VMEM((left_rows, LANES), jnp.float32),
                pltpu.VMEM((left_rows, LANES), jnp.float32),
            ],
        ),
        out_shape=[
            jax.ShapeDtypeStruct((pairs, 1, left_rows), jnp.float32),
            jax.ShapeDtypeStruct((pairs, 1, right_rows), jnp.float32),
        ],
        compiler_params=pltpu.CompilerParams(vmem_limit_bytes=32 << 20),
        cost_estimate=pl.CostEstimate(
            flops=2 * pairs * left_rows * right_rows * width,
            bytes_accessed=2 * (pairs + 1) * right_rows * width,
            transcendentals=2 * pairs * left_rows * right_rows,
        ),
    )(meta, left, right)
    return rows[:, 0], cols[:, 0]


def after(value, *earlier):
    return lax.optimization_barrier((value, *earlier))[0]


def shards(embeddings, lengths):
    answers, length, _ = embeddings.shape
    count = lax.axis_size("cand")
    here = lax.axis_index("cand")
    is_even = here % 2 == 0

    first_to = [(i, (i - 2 if i % 2 == 0 else i + 2) % count) for i in range(count)]
    second_to = [(i, (i - 1 if i % 2 == 0 else i + 1) % count) for i in range(count)]
    mate_to = [(i, i ^ 1) for i in range(count)]

    def move(value, pairs):
        return lax.ppermute(value, "cand", pairs)

    def back(value, pairs):
        return lax.ppermute(value, "cand", [(b, a) for a, b in pairs])

    first = move(packet_of(embeddings[0], lengths[0]), first_to)
    unit = make_unit(embeddings, lengths)
    mate_unit = move(unit, mate_to)
    residents = jnp.concatenate([unit, mate_unit])

    every = jnp.arange(2 * answers, dtype=jnp.int32)
    nothing = jnp.zeros_like(every)
    first_meta = jnp.stack([nothing, every, (is_even | (every < answers)).astype(jnp.int32)])
    second_meta = jnp.stack([nothing, every, (~is_even | (every >= answers)).astype(jnp.int32)])
    inner_meta = jnp.where(
        is_even,
        jnp.array([[0, 0, 0], [1, 2, 3], [1, 1, 1]], jnp.int32),
        jnp.array([[0, 3, 3], [1, 0, 1], [1, 1, 1]], jnp.int32),
    )
    rows, cols = match_pairs(inner_meta, residents, residents, False)
    zero = jnp.zeros_like(rows[0])
    totals = jnp.where(
        is_even,
        jnp.stack([rows[0] + rows[1] + rows[2], cols[0], cols[1], cols[2]]),
        jnp.stack([rows[0] + cols[1], cols[0] + cols[2], zero, rows[1] + rows[2]]),
    )

    second = move(after(packet_of(embeddings[1], lengths[1]), rows), second_to)
    rows, cols = match_pairs(first_meta, first, residents, True)
    totals = totals + cols
    first_back = back(jnp.sum(rows, axis=0), first_to)
    rows, cols = match_pairs(second_meta, second, residents, True)
    totals = totals + cols
    second_back = back(jnp.sum(rows, axis=0), second_to)
    mate_back = move(totals[answers:], mate_to)

    consensus = totals[:answers] + mate_back + jnp.stack([first_back, second_back])
    inside = lax.broadcasted_iota(jnp.int32, (answers, length), 1) < lengths[:, None]
    return jnp.where(inside, consensus / (answers - 1 + 4 * answers), 0.0)


def solution(mesh):
    return jax.shard_map(
        shards,
        mesh=mesh,
        in_specs=(P(("group", "cand"), None, None), P(("group", "cand"))),
        out_specs=P(("group", "cand"), None),
        check_vma=False,
    )
```

```python
import functools

import jax
import jax.numpy as jnp
from jax import lax
from jax.experimental import pallas as pl
from jax.experimental.pallas import tpu as pltpu
from jax.sharding import PartitionSpec as P

SCALE = 256.0 * 1.4426950408889634
LOWEST = -1e30
LANES = 128
TAG_ROWS = 16
TAG_BASE = 64
ROW_TILE = 1024
COL_TILE = 512
SUM_TILE = 256
SUM_STEP = 64


def unit_rows(embeddings):
    values = embeddings.astype(jnp.float32)
    scale = lax.rsqrt(jnp.sum(values * values, axis=-1, keepdims=True) + 1e-06)
    return (values * scale).astype(jnp.bfloat16)


def length_of(tag):
    return tag[0, 0].astype(jnp.int32) * TAG_BASE + tag[TAG_ROWS - 1, 0].astype(jnp.int32)


def packet_kernel(lengths, values_ref, *refs, slot, rows):
    unit_ref = refs[-1]
    tile = unit_ref.shape[1]
    unit = unit_rows(values_ref[0])
    row = lax.broadcasted_iota(jnp.int32, unit.shape, 0) + pl.program_id(0) * tile
    high = lengths[slot] // TAG_BASE
    low = lengths[slot] % TAG_BASE
    tag = jnp.where(row < rows + TAG_ROWS // 2, high, low).astype(jnp.float32)
    unit_ref[0] = jnp.where(row < rows, unit.astype(jnp.float32), tag).astype(jnp.bfloat16)


def packet_of(embeddings, lengths, slot, *earlier):
    _, rows, width = embeddings.shape
    whole = rows + TAG_ROWS
    steps = max(n for n in range(1, 9) if whole % (n * TAG_ROWS) == 0)
    tile = whole // steps
    return pl.pallas_call(
        functools.partial(packet_kernel, slot=slot, rows=rows),
        grid_spec=pltpu.PrefetchScalarGridSpec(
            num_scalar_prefetch=1,
            grid=(steps,),
            in_specs=[pl.BlockSpec((1, tile, width), lambda i, m: (slot, i, 0))]
            + [pl.BlockSpec(memory_space=pl.ANY)] * len(earlier),
            out_specs=pl.BlockSpec((1, tile, width), lambda i, m: (0, i, 0)),
        ),
        out_shape=jax.ShapeDtypeStruct((1, whole, width), jnp.bfloat16),
    )(lengths, embeddings, *earlier)


def pass_kernel(*refs):
    del refs


def after(value, *earlier):
    spec = pl.BlockSpec(memory_space=pl.ANY)
    return pl.pallas_call(
        pass_kernel,
        in_specs=[spec] * (1 + len(earlier)),
        out_specs=spec,
        out_shape=jax.ShapeDtypeStruct(value.shape, value.dtype),
        input_output_aliases={0: 0},
    )(value, *earlier)


def pair_kernel(meta, left_ref, right_ref, peak_in, sum_in, row_ref, peak_ref, sum_ref, scores, peak, total):
    pair = pl.program_id(0)
    left_rows = scores.shape[0]
    right_rows = scores.shape[1]
    left_len = meta[2, pair]
    right_len = meta[3, pair]
    row_tile = min(ROW_TILE, left_rows)
    col_tile = min(COL_TILE, right_rows)
    sum_rows = min(SUM_TILE, left_rows)
    sum_cols = min(SUM_TILE, right_rows)

    row_ref[...] = jnp.zeros_like(row_ref)
    peak_ref[...] = peak_in[...]
    sum_ref[...] = sum_in[...]

    def at(index, size):
        return pl.ds(pl.multiple_of(index * size, size), size)

    def steps(count, size):
        return lax.div(count + size - 1, size)

    @pl.when((left_len > 0) & (right_len > 0))
    def _():
        peak[...] = jnp.full_like(peak, LOWEST)
        total[...] = jnp.zeros_like(total)

        def score_cols(j, carry):
            cols = at(j, col_tile)
            right = right_ref[0, cols, :]
            col_at = lax.broadcasted_iota(jnp.int32, (1, col_tile), 1) + j * col_tile
            col_bias = jnp.where(col_at < right_len, 0.0, LOWEST)

            def score_rows(i, col_peak):
                rows = at(i, row_tile)
                tile = lax.dot_general(
                    left_ref[0, rows, :], right, (((1,), (1,)), ((), ())), preferred_element_type=jnp.float32
                )
                row_at = lax.broadcasted_iota(jnp.int32, (row_tile, 1), 0) + i * row_tile
                row_bias = jnp.where(row_at < left_len, 0.0, LOWEST)
                tile = (tile * SCALE + col_bias) + row_bias
                scores[rows, cols] = tile
                row_peak = peak[rows, :]
                for k in range(0, col_tile, LANES):
                    row_peak = jnp.maximum(row_peak, tile[:, k : k + LANES])
                peak[rows, :] = row_peak
                folded = jnp.max(tile.reshape(row_tile // 8, 8, col_tile), axis=0)
                return jnp.maximum(col_peak, folded)

            col_peak = lax.fori_loop(
                0, steps(left_len, row_tile), score_rows, jnp.full((8, col_tile), LOWEST, jnp.float32)
            )
            peak_ref[0, :, cols] = jnp.maximum(peak_in[0, :, cols], jnp.max(col_peak, axis=0, keepdims=True))
            return carry

        lax.fori_loop(0, steps(right_len, col_tile), score_cols, 0)

        def sum_cols_of(j, carry):
            cols = at(j, sum_cols)
            col_peak = peak_ref[0, :, cols]

            def sum_rows_of(i, col_sum):
                for step in range(0, sum_rows, SUM_STEP):
                    rows = pl.ds(pl.multiple_of(i * sum_rows, sum_rows) + step, SUM_STEP)
                    tile = scores[rows, cols]
                    row_peak = peak[rows, :]
                    row_sum = total[rows, :]
                    for k in range(0, sum_cols, LANES):
                        row_sum = row_sum + jnp.exp2(tile[:, k : k + LANES] - row_peak)
                    total[rows, :] = row_sum
                    terms = jnp.exp2(tile - col_peak)
                    col_sum = col_sum + jnp.sum(terms.reshape(SUM_STEP // 8, 8, sum_cols), axis=0)
                return col_sum

            col_sum = lax.fori_loop(
                0, steps(left_len, sum_rows), sum_rows_of, jnp.zeros((8, sum_cols), jnp.float32)
            )
            earlier = sum_in[0, :, cols] * jnp.exp2(peak_in[0, :, cols] - col_peak)
            sum_ref[0, :, cols] = earlier + jnp.sum(col_sum, axis=0, keepdims=True)
            return carry

        lax.fori_loop(0, steps(right_len, sum_cols), sum_cols_of, 0)

        def finish_rows(i, carry):
            rows = at(i, sum_rows)
            lane_peak = jnp.transpose(peak[rows, :])
            lane_sum = jnp.transpose(total[rows, :])
            row_peak = jnp.max(lane_peak, axis=0, keepdims=True)
            row_sum = jnp.sum(lane_sum * jnp.exp2(lane_peak - row_peak), axis=0, keepdims=True)
            row_ref[0, :, rows] = (row_peak + jnp.log2(row_sum)) * (1.0 / SCALE)
            return carry

        lax.fori_loop(0, steps(left_len, sum_rows), finish_rows, 0)


def match_pairs(meta, left, left_rows, right, peaks=None, sums=None):
    pairs = meta.shape[1]
    width = left.shape[2]
    right_rows = right.shape[1] - TAG_ROWS
    if peaks is None:
        peaks = jnp.full((pairs, 1, right_rows), LOWEST, jnp.float32)
        sums = jnp.zeros((pairs, 1, right_rows), jnp.float32)
    row_spec = pl.BlockSpec((1, 1, left_rows), lambda p, m: (p, 0, 0))
    col_spec = pl.BlockSpec((1, 1, right_rows), lambda p, m: (p, 0, 0))
    col_shape = jax.ShapeDtypeStruct((pairs, 1, right_rows), jnp.float32)
    return pl.pallas_call(
        pair_kernel,
        grid_spec=pltpu.PrefetchScalarGridSpec(
            num_scalar_prefetch=1,
            grid=(pairs,),
            in_specs=[
                pl.BlockSpec((1,) + left.shape[1:], lambda p, m: (m[0, p], 0, 0)),
                pl.BlockSpec((1,) + right.shape[1:], lambda p, m: (m[1, p], 0, 0)),
                col_spec,
                col_spec,
            ],
            out_specs=[row_spec, col_spec, col_spec],
            scratch_shapes=[
                pltpu.VMEM((left_rows, right_rows), jnp.float32),
                pltpu.VMEM((left_rows, LANES), jnp.float32),
                pltpu.VMEM((left_rows, LANES), jnp.float32),
            ],
        ),
        out_shape=[jax.ShapeDtypeStruct((pairs, 1, left_rows), jnp.float32), col_shape, col_shape],
        compiler_params=pltpu.CompilerParams(vmem_limit_bytes=32 << 20),
        cost_estimate=pl.CostEstimate(
            flops=2 * pairs * left_rows * right_rows * width,
            bytes_accessed=2 * (pairs + 1) * right_rows * width,
            transcendentals=2 * pairs * left_rows * right_rows,
        ),
    )(meta, left, right, peaks, sums)


def matches_of(meta, peaks, sums):
    return jnp.where(meta[3][:, None] > 0, (peaks + jnp.log2(sums))[:, 0] * (1.0 / SCALE), 0.0)


def shards(embeddings, lengths):
    answers, length, _ = embeddings.shape
    count = lax.axis_size("cand")
    is_even = lax.axis_index("cand") % 2 == 0

    first_to = [(i, (i - 2 if i % 2 == 0 else i + 2) % count) for i in range(count)]
    second_to = [(i, (i - 1 if i % 2 == 0 else i + 1) % count) for i in range(count)]
    mate_to = [(i, i ^ 1) for i in range(count)]

    def move(value, pairs):
        return lax.ppermute(value, "cand", pairs)

    def back(value, pairs):
        return lax.ppermute(value, "cand", [(b, a) for a, b in pairs])

    own_first = packet_of(embeddings, lengths, 0)
    first = move(own_first, first_to)
    own_second = packet_of(embeddings, lengths, 1, own_first)
    unit = jnp.concatenate([own_first, own_second])
    mate_unit = move(unit, mate_to)
    residents = jnp.concatenate([unit, mate_unit])
    near = jnp.concatenate([lengths, jnp.stack([length_of(mate_unit[k, length:]) for k in range(answers)])])

    every = jnp.arange(2 * answers, dtype=jnp.int32)
    nothing = jnp.zeros_like(every)

    def arrival_meta(left_len, active):
        return jnp.stack([nothing, every, jnp.broadcast_to(left_len, every.shape), jnp.where(active, near, 0)])

    inner_left = jnp.where(is_even, jnp.array([0, 0, 0]), jnp.array([0, 3, 3]))
    inner_right = jnp.where(is_even, jnp.array([1, 2, 3]), jnp.array([1, 0, 1]))
    inner_meta = jnp.stack([inner_left, inner_right, near[inner_left], near[inner_right]]).astype(jnp.int32)
    rows, peaks, sums = match_pairs(inner_meta, residents, length, residents)
    rows = rows[:, 0]
    cols = matches_of(inner_meta, peaks, sums)
    zero = jnp.zeros_like(rows[0])
    totals = jnp.where(
        is_even,
        jnp.stack([rows[0] + rows[1] + rows[2], cols[0], cols[1], cols[2]]),
        jnp.stack([rows[0] + cols[1], cols[0] + cols[2], zero, rows[1] + rows[2]]),
    )

    half = length // 2
    lower = after(jnp.concatenate([own_second[:, :half], own_second[:, length:]], axis=1), first, rows)
    lower = move(lower, second_to)
    first_meta = arrival_meta(length_of(first[0, length:]), is_even | (every < answers))
    rows, peaks, sums = match_pairs(first_meta, first, length, residents)
    totals = totals + matches_of(first_meta, peaks, sums)
    upper = move(after(own_second[:, half:length], rows), second_to)
    first_back = back(jnp.sum(rows[:, 0], axis=0), first_to)

    second_len = length_of(lower[0, half:])
    second_near = ~is_even | (every >= answers)
    second_meta = arrival_meta(jnp.minimum(second_len, half), second_near)
    lower_rows, peaks, sums = match_pairs(second_meta, lower, half, residents)
    second_meta = arrival_meta(jnp.maximum(second_len - half, 0), second_near)
    upper_rows, peaks, sums = match_pairs(second_meta, upper, length - half, residents, peaks, sums)
    totals = totals + matches_of(second_meta, peaks, sums)
    second_rows = jnp.concatenate([jnp.sum(lower_rows[:, 0], axis=0), jnp.sum(upper_rows[:, 0], axis=0)])
    second_back = back(second_rows, second_to)
    mate_back = move(totals[answers:], mate_to)

    consensus = totals[:answers] + mate_back + jnp.stack([first_back, second_back])
    inside = lax.broadcasted_iota(jnp.int32, (answers, length), 1) < lengths[:, None]
    return jnp.where(inside, consensus / (answers - 1 + 4 * answers), 0.0)


def solution(mesh):
    return jax.shard_map(
        shards,
        mesh=mesh,
        in_specs=(P(("group", "cand"), None, None), P(("group", "cand"))),
        out_specs=P(("group", "cand"), None),
        check_vma=False,
    )
```

```python
import functools

import jax
import jax.numpy as jnp
from jax import lax
from jax.experimental import pallas as pl
from jax.experimental.pallas import tpu as pltpu
from jax.sharding import PartitionSpec as P

SCALE = 256.0 * 1.4426950408889634
LOWEST = -1e30
LANES = 128
TAG_ROWS = 16
TAG_BASE = 64
ROW_TILE = 512
COL_TILE = 512
SUM_STEP = 64
CHUNKS = 4
SMALL_COST = pl.CostEstimate(flops=1, bytes_accessed=1, transcendentals=0)


def unit_rows(embeddings):
    values = embeddings.astype(jnp.float32)
    scale = lax.rsqrt(jnp.sum(values * values, axis=-1, keepdims=True) + 1e-06)
    return (values * scale).astype(jnp.bfloat16)


def length_of(tag):
    values = tag.astype(jnp.float32)
    upper = lax.broadcasted_iota(jnp.int32, values.shape, 0) < TAG_ROWS // 2
    high = jnp.max(jnp.where(upper, values, 0.0)).astype(jnp.int32)
    low = jnp.max(jnp.where(upper, 0.0, values)).astype(jnp.int32)
    return high * TAG_BASE + low


def packet_kernel(lengths, values_ref, *refs, slot, rows):
    packet_ref, values_buf, packet_buf, in_sem, out_sem = refs[-5:]
    chunk = rows // CHUNKS
    tags = pl.ds(rows, TAG_ROWS)

    def copy_in(k):
        at = pl.ds(k * chunk, chunk)
        return pltpu.make_async_copy(values_ref.at[slot, at, :], values_buf.at[at, :], in_sem.at[k])

    def copy_out(k):
        at = pl.ds(k * chunk, chunk)
        return pltpu.make_async_copy(packet_buf.at[at, :], packet_ref.at[0, at, :], out_sem.at[k])

    for k in range(CHUNKS):
        copy_in(k).start()
    shape = (TAG_ROWS, values_buf.shape[1])
    upper = lax.broadcasted_iota(jnp.int32, shape, 0) < TAG_ROWS // 2
    tag = jnp.where(upper, lengths[slot] // TAG_BASE, lengths[slot] % TAG_BASE)
    packet_buf[tags, :] = tag.astype(jnp.float32).astype(jnp.bfloat16)
    tag_out = pltpu.make_async_copy(packet_buf.at[tags, :], packet_ref.at[0, tags, :], out_sem.at[CHUNKS])
    tag_out.start()
    for k in range(CHUNKS):
        copy_in(k).wait()
        at = pl.ds(k * chunk, chunk)
        packet_buf[at, :] = unit_rows(values_buf[at, :])
        copy_out(k).start()
    for k in range(CHUNKS):
        copy_out(k).wait()
    tag_out.wait()


def packet_of(embeddings, lengths, slot, *earlier):
    _, rows, width = embeddings.shape
    whole = rows + TAG_ROWS
    anywhere = pl.BlockSpec(memory_space=pl.ANY)
    return pl.pallas_call(
        functools.partial(packet_kernel, slot=slot, rows=rows),
        grid_spec=pltpu.PrefetchScalarGridSpec(
            num_scalar_prefetch=1,
            grid=(1,),
            in_specs=[anywhere] * (1 + len(earlier)),
            out_specs=anywhere,
            scratch_shapes=[
                pltpu.VMEM((rows, width), jnp.bfloat16),
                pltpu.VMEM((whole, width), jnp.bfloat16),
                pltpu.SemaphoreType.DMA((CHUNKS,)),
                pltpu.SemaphoreType.DMA((CHUNKS + 1,)),
            ],
        ),
        out_shape=jax.ShapeDtypeStruct((1, whole, width), jnp.bfloat16),
        compiler_params=pltpu.CompilerParams(vmem_limit_bytes=60 << 20),
        cost_estimate=SMALL_COST,
    )(lengths, embeddings, *earlier)


def pass_kernel(*refs):
    del refs


def after(value, *earlier):
    spec = pl.BlockSpec(memory_space=pl.ANY)
    return pl.pallas_call(
        pass_kernel,
        in_specs=[spec] * (1 + len(earlier)),
        out_specs=spec,
        out_shape=jax.ShapeDtypeStruct(value.shape, value.dtype),
        input_output_aliases={0: 0},
        cost_estimate=SMALL_COST,
    )(value, *earlier)


def match_kernel(meta, *refs, lefts, rights, offset):
    left_refs = refs[:lefts]
    tag_refs = refs[lefts : 2 * lefts]
    right_refs = refs[2 * lefts : 2 * lefts + rights]
    peak_in, sum_in, row_ref, peak_ref, sum_ref = refs[2 * lefts + rights : 2 * lefts + rights + 5]
    (left_buf, left_tags, right_buf, scores_even, scores_odd, rows_even, rows_odd, cols_even, cols_odd, base, total,
     items, waiting, left_sem, tag_sem, right_sem) = refs[2 * lefts + rights + 5 :]
    row_tile, col_tile = scores_even.shape
    left_rows = left_buf.shape[1]
    right_rows = peak_ref.shape[2]
    most = (meta.shape[0] - 1) // 2
    pairs = meta[0]

    def left_copy(k):
        return pltpu.make_async_copy(left_refs[k].at[0, pl.ds(0, left_rows), :], left_buf.at[k], left_sem.at[k])

    def tag_copy(k):
        tag_at = tag_refs[k].shape[1] - TAG_ROWS
        return pltpu.make_async_copy(tag_refs[k].at[0, pl.ds(tag_at, TAG_ROWS), :], left_tags.at[k], tag_sem.at[k])

    def right_tag_copy(k):
        return pltpu.make_async_copy(
            right_refs[k].at[0, pl.ds(right_rows, TAG_ROWS), :], left_tags.at[lefts + k], tag_sem.at[lefts + k]
        )

    def right_copy(k):
        return pltpu.make_async_copy(right_refs[k].at[0, pl.ds(0, right_rows), :], right_buf.at[k], right_sem.at[k])

    for k in range(lefts):
        tag_copy(k).start()
    for k in range(rights):
        right_tag_copy(k).start()
    def fetch(p):
        for k in range(rights):

            @pl.when((p < pairs) & (meta[1 + most + jnp.minimum(p, most - 1)] == k))
            def _():
                right_copy(k).start()

    left_copy(0).start()
    fetch(0)
    for k in range(1, lefts):
        left_copy(k).start()
    waiting[0] = 0

    row_ref[...] = jnp.zeros_like(row_ref)
    peak_ref[...] = peak_in[...]
    sum_ref[...] = sum_in[...]
    for k in range(lefts):
        tag_copy(k).wait()
    for k in range(rights):
        right_tag_copy(k).wait()
    left_lens = [jnp.clip(length_of(left_tags[k]) - offset, 0, left_rows) for k in range(lefts)]
    right_lens = [length_of(left_tags[lefts + k]) for k in range(rights)]

    def pick(values, index):
        found = values[0]
        for k in range(1, len(values)):
            found = jnp.where(index == k, values[k], found)
        return found

    def list_pair(p, n):
        left = meta[1 + p]
        right = meta[1 + most + p]
        left_len = pick(left_lens, left)
        right_len = pick(right_lens, right)
        down = lax.div(left_len + row_tile - 1, row_tile)
        across = lax.div(right_len + col_tile - 1, col_tile)

        def list_tile(t, n):
            i = lax.div(t, across)
            j = lax.rem(t, across)
            items[0, n] = left
            items[1, n] = right
            items[2, n] = i
            items[3, n] = j
            items[4, n] = left_len - i * row_tile
            items[5, n] = right_len - j * col_tile
            items[6, n] = (j == 0).astype(jnp.int32)
            items[7, n] = (j == across - 1).astype(jnp.int32)
            items[8, n] = p
            return n + 1

        return lax.fori_loop(0, down * across, list_tile, n)

    count = lax.fori_loop(0, pairs, list_pair, 0)
    for k in range(lefts):
        left_copy(k).wait()

    def at(index, size):
        return pl.ds(pl.multiple_of(index * size, size), size)

    def score(item, scores, rows_now, rows_before, cols_now):
        left = items[0, item]
        right = items[1, item]
        rows = at(items[2, item], row_tile)
        cols = at(items[3, item], col_tile)
        row_left = items[4, item]
        col_left = items[5, item]
        first = items[6, item] > 0
        col_bias = jnp.where(lax.broadcasted_iota(jnp.int32, (1, col_tile), 1) < col_left, 0.0, LOWEST)
        row_bias = jnp.where(lax.broadcasted_iota(jnp.int32, (row_tile, 1), 0) < row_left, 0.0, LOWEST)
        tile = lax.dot_general(
            left_buf[left, rows, :], right_buf[right, cols, :], (((1,), (1,)), ((), ())),
            preferred_element_type=jnp.float32,
        )
        tile = (tile * SCALE + col_bias) + row_bias
        scores[...] = tile
        row_peak = jnp.where(first, LOWEST, rows_before[...])
        for k in range(0, col_tile, LANES):
            row_peak = jnp.maximum(row_peak, tile[:, k : k + LANES])
        rows_now[...] = row_peak
        old = peak_ref[right, :, cols]
        new = jnp.maximum(old, jnp.max(tile, axis=0, keepdims=True))
        cols_now[0:1, :] = old
        cols_now[1:2, :] = new
        peak_ref[right, :, cols] = new

    def add(item, real, scores, rows_now, cols_now):
        right = items[1, item]
        cols = at(items[3, item], col_tile)
        first = items[6, item] > 0
        old = cols_now[0:1, :]
        new = cols_now[1:2, :]
        col_sum = jnp.zeros((8, col_tile), jnp.float32)
        for start in range(0, row_tile, SUM_STEP):
            rows = pl.ds(start, SUM_STEP)
            tile = scores[rows, :]
            row_peak = rows_now[rows, :]
            row_sum = total[rows, :] * jnp.exp2(base[rows, :] - row_peak)
            row_sum = jnp.where(first, 0.0, row_sum)
            for k in range(0, col_tile, LANES):
                row_sum = row_sum + jnp.exp2(tile[:, k : k + LANES] - row_peak)
            total[rows, :] = row_sum
            base[rows, :] = row_peak
            terms = jnp.exp2(tile - new)
            col_sum = col_sum + jnp.sum(terms.reshape(SUM_STEP // 8, 8, col_tile), axis=0)
        before = sum_ref[right, :, cols]
        after_sum = before * jnp.exp2(old - new) + jnp.sum(col_sum, axis=0, keepdims=True)
        sum_ref[right, :, cols] = jnp.where(real, after_sum, before)

    def finish(item, real):
        @pl.when(real & (items[7, item] > 0))
        def _():
            left = items[0, item]
            lane_peak = jnp.transpose(base[...])
            lane_sum = jnp.transpose(total[...])
            row_peak = jnp.max(lane_peak, axis=0, keepdims=True)
            row_sum = jnp.sum(lane_sum * jnp.exp2(lane_peak - row_peak), axis=0, keepdims=True)
            rows = at(items[2, item], row_tile)
            row_ref[left, :, rows] = row_ref[left, :, rows] + (row_peak + jnp.log2(row_sum)) * (1.0 / SCALE)

    def ready(item):
        pair = items[8, item]

        @pl.when(waiting[0] <= pair)
        def _():
            fetch(pair + 1)
            right = items[1, item]
            for k in range(rights):

                @pl.when(right == k)
                def _():
                    right_copy(k).wait()

            waiting[0] = pair + 1

    @pl.when(count == 0)
    def _():
        for k in range(rights):

            @pl.when(meta[1 + most] == k)
            def _():
                right_copy(k).wait()

    @pl.when(count > 0)
    def _():
        def two(t, carry):
            before = jnp.maximum(2 * t - 1, 0)
            even = jnp.minimum(2 * t, count - 1)
            odd = jnp.minimum(2 * t + 1, count - 1)
            ready(even)
            was_real = (t > 0) & (2 * t - 1 < count)
            add(jnp.minimum(before, count - 1), was_real, scores_odd, rows_odd, cols_odd)
            score(even, scores_even, rows_even, rows_odd, cols_even)
            finish(jnp.minimum(before, count - 1), was_real)
            ready(odd)
            is_real = 2 * t < count
            add(even, is_real, scores_even, rows_even, cols_even)
            score(odd, scores_odd, rows_odd, rows_even, cols_odd)
            finish(even, is_real)
            return carry

        lax.fori_loop(0, lax.div(count, 2) + 1, two, 0)


def match(meta, lefts, left_rows, rights, tags=None, offset=0, carried=None):
    tags = lefts if tags is None else tags
    count = len(rights)
    _, whole, width = rights[0].shape
    right_rows = whole - TAG_ROWS
    row_tile = min(ROW_TILE, left_rows)
    col_tile = min(COL_TILE, right_rows)
    most = (meta.shape[0] - 1) // 2
    tiles = most * (left_rows // row_tile) * (right_rows // col_tile)
    if carried is None:
        carried = (
            jnp.full((count, 1, right_rows), LOWEST, jnp.float32),
            jnp.zeros((count, 1, right_rows), jnp.float32),
        )
    anywhere = pl.BlockSpec(memory_space=pl.ANY)
    row_shape = (len(lefts), 1, left_rows)
    col_shape = (count, 1, right_rows)
    row_spec = pl.BlockSpec(row_shape, lambda p, m: (0, 0, 0))
    col_spec = pl.BlockSpec(col_shape, lambda p, m: (0, 0, 0))
    rows, peaks, sums = pl.pallas_call(
        functools.partial(match_kernel, lefts=len(lefts), rights=count, offset=offset),
        grid_spec=pltpu.PrefetchScalarGridSpec(
            num_scalar_prefetch=1,
            grid=(1,),
            in_specs=[anywhere] * (2 * len(lefts) + count) + [col_spec, col_spec],
            out_specs=[row_spec, col_spec, col_spec],
            scratch_shapes=[
                pltpu.VMEM((len(lefts), left_rows, width), jnp.bfloat16),
                pltpu.VMEM((len(lefts) + count, TAG_ROWS, width), jnp.bfloat16),
                pltpu.VMEM((count, right_rows, width), jnp.bfloat16),
                pltpu.VMEM((row_tile, col_tile), jnp.float32),
                pltpu.VMEM((row_tile, col_tile), jnp.float32),
                pltpu.VMEM((row_tile, LANES), jnp.float32),
                pltpu.VMEM((row_tile, LANES), jnp.float32),
                pltpu.VMEM((8, col_tile), jnp.float32),
                pltpu.VMEM((8, col_tile), jnp.float32),
                pltpu.VMEM((row_tile, LANES), jnp.float32),
                pltpu.VMEM((row_tile, LANES), jnp.float32),
                pltpu.SMEM((9, tiles), jnp.int32),
                pltpu.SMEM((1,), jnp.int32),
                pltpu.SemaphoreType.DMA((len(lefts),)),
                pltpu.SemaphoreType.DMA((len(lefts) + count,)),
                pltpu.SemaphoreType.DMA((count,)),
            ],
        ),
        out_shape=[
            jax.ShapeDtypeStruct(row_shape, jnp.float32),
            jax.ShapeDtypeStruct(col_shape, jnp.float32),
            jax.ShapeDtypeStruct(col_shape, jnp.float32),
        ],
        compiler_params=pltpu.CompilerParams(vmem_limit_bytes=32 << 20),
        cost_estimate=SMALL_COST,
    )(meta, *lefts, *tags, *rights, *carried)
    return rows[:, 0], (peaks, sums)


def matches_of(active, carried):
    peaks, sums = carried
    return jnp.where(active[:, None], (peaks + jnp.log2(sums))[:, 0] * (1.0 / SCALE), 0.0)


def shards(embeddings, lengths):
    answers, length, _ = embeddings.shape
    count = lax.axis_size("cand")
    is_even = lax.axis_index("cand") % 2 == 0

    first_to = [(i, (i - 2 if i % 2 == 0 else i + 2) % count) for i in range(count)]
    second_to = [(i, (i - 1 if i % 2 == 0 else i + 1) % count) for i in range(count)]
    mate_to = [(i, i ^ 1) for i in range(count)]

    def move(value, pairs):
        return lax.ppermute(value, "cand", pairs)

    def back(value, pairs):
        return lax.ppermute(value, "cand", [(b, a) for a, b in pairs])

    def by_role(even, odd):
        return jnp.where(is_even, jnp.array(even, jnp.int32), jnp.array(odd, jnp.int32))

    own_first = packet_of(embeddings, lengths, 0)
    first = move(own_first, first_to)
    own_second = packet_of(embeddings, lengths, 1, own_first)
    mate_first = move(own_first, mate_to)
    mate_second = move(own_second, mate_to)
    near = [own_first, own_second, mate_first, mate_second]
    every = jnp.arange(2 * answers)

    inner_meta = by_role([3, 0, 0, 0, 1, 2, 3], [3, 0, 2, 1, 1, 0, 3])
    inner_rows, inner_cols = match(inner_meta, [own_first, own_second, mate_second], length, near)

    half = length // 2
    lower = jnp.concatenate([own_second[:, :half], own_second[:, length:]], axis=1)
    lower = move(after(lower, inner_rows), second_to)
    upper = move(after(own_second[:, half:length], first), second_to)
    first_meta = by_role([4, 0, 0, 0, 0, 0, 1, 2, 3], [2, 0, 0, 0, 0, 0, 1, 1, 1])
    first_rows, first_cols = match(first_meta, [first], length, near)
    first_back = back(first_rows[0], first_to)
    second_meta = by_role([2, 0, 0, 0, 0, 2, 3, 3, 3], [4, 0, 0, 0, 0, 0, 1, 2, 3])
    lower_rows, second_cols = match(second_meta, [lower], half, near)
    upper_rows, second_cols = match(
        second_meta, [upper], length - half, near, tags=[lower], offset=half, carried=second_cols
    )
    second_back = back(jnp.concatenate([lower_rows[0], upper_rows[0]]), second_to)

    zero = jnp.zeros_like(inner_rows[0])
    totals = jnp.stack([inner_rows[0], inner_rows[1], zero, inner_rows[2]])
    totals = totals + matches_of(jnp.where(is_even, every > 0, every != 2), inner_cols)
    totals = totals + matches_of(is_even | (every < answers), first_cols)
    totals = totals + matches_of(~is_even | (every >= answers), second_cols)
    mate_back = move(totals[answers:], mate_to)

    consensus = totals[:answers] + mate_back + jnp.stack([first_back, second_back])
    inside = lax.broadcasted_iota(jnp.int32, (answers, length), 1) < lengths[:, None]
    return jnp.where(inside, consensus / (answers - 1 + 4 * answers), 0.0)


def solution(mesh):
    return jax.shard_map(
        shards,
        mesh=mesh,
        in_specs=(P(("group", "cand"), None, None), P(("group", "cand"))),
        out_specs=P(("group", "cand"), None),
        check_vma=False,
    )
```

```python
import functools

import jax
import jax.numpy as jnp
from jax import lax
from jax.experimental import pallas as pl
from jax.experimental.pallas import tpu as pltpu
from jax.sharding import PartitionSpec as P

SCALE = 256.0 * 1.4426950408889634
LOWEST = -1e30
LANES = 128
TAG_ROWS = 16
TAG_BASE = 64
ROW_TILE = 512
COL_TILE = 256
SUM_STEP = 64
CHUNKS = 4
SMALL_COST = pl.CostEstimate(flops=1, bytes_accessed=1, transcendentals=0)


def unit_rows(embeddings):
    values = embeddings.astype(jnp.float32)
    scale = lax.rsqrt(jnp.sum(values * values, axis=-1, keepdims=True) + 1e-06)
    return (values * scale).astype(jnp.bfloat16)


def length_of(tag):
    values = tag.astype(jnp.float32)
    upper = lax.broadcasted_iota(jnp.int32, values.shape, 0) < TAG_ROWS // 2
    high = jnp.max(jnp.where(upper, values, 0.0)).astype(jnp.int32)
    low = jnp.max(jnp.where(upper, 0.0, values)).astype(jnp.int32)
    return high * TAG_BASE + low


def packet_kernel(lengths, values_ref, *refs, slot, rows, outs):
    packet_refs = refs[-outs - 4 : -4]
    values_buf, packet_buf, in_sem, out_sem = refs[-4:]
    chunk = rows // CHUNKS
    tags = pl.ds(rows, TAG_ROWS)
    parts = [packet_ref.shape[1] - TAG_ROWS for packet_ref in packet_refs]
    starts = [sum(parts[:k]) % rows for k in range(outs)]

    def copy_in(k):
        at = pl.ds(k * chunk, chunk)
        return pltpu.make_async_copy(values_ref.at[slot, at, :], values_buf.at[at, :], in_sem.at[k])

    def tag_out(k):
        to = packet_refs[k].at[0, pl.ds(parts[k], TAG_ROWS), :]
        return pltpu.make_async_copy(packet_buf.at[tags, :], to, out_sem.at[k, CHUNKS])

    def copies_out(c):
        copies = []
        for k in range(outs):
            offset = c * chunk - starts[k]
            if 0 <= offset < parts[k]:
                to = packet_refs[k].at[0, pl.ds(offset, chunk), :]
                copies.append(pltpu.make_async_copy(packet_buf.at[pl.ds(c * chunk, chunk), :], to, out_sem.at[k, c]))
        return copies

    for c in range(CHUNKS):
        copy_in(c).start()
    shape = (TAG_ROWS, values_buf.shape[1])
    upper = lax.broadcasted_iota(jnp.int32, shape, 0) < TAG_ROWS // 2
    tag = jnp.where(upper, lengths[slot] // TAG_BASE, lengths[slot] % TAG_BASE)
    packet_buf[tags, :] = tag.astype(jnp.float32).astype(jnp.bfloat16)
    for k in range(outs):
        tag_out(k).start()
    for c in range(CHUNKS):
        copy_in(c).wait()
        at = pl.ds(c * chunk, chunk)
        packet_buf[at, :] = unit_rows(values_buf[at, :])
        for copy in copies_out(c):
            copy.start()
    for c in range(CHUNKS):
        for copy in copies_out(c):
            copy.wait()
    for k in range(outs):
        tag_out(k).wait()


def packets_of(embeddings, lengths, slot, parts, *earlier):
    _, rows, width = embeddings.shape
    anywhere = pl.BlockSpec(memory_space=pl.ANY)
    return pl.pallas_call(
        functools.partial(packet_kernel, slot=slot, rows=rows, outs=len(parts)),
        grid_spec=pltpu.PrefetchScalarGridSpec(
            num_scalar_prefetch=1,
            grid=(1,),
            in_specs=[anywhere] * (1 + len(earlier)),
            out_specs=[anywhere] * len(parts),
            scratch_shapes=[
                pltpu.VMEM((rows, width), jnp.bfloat16),
                pltpu.VMEM((rows + TAG_ROWS, width), jnp.bfloat16),
                pltpu.SemaphoreType.DMA((CHUNKS,)),
                pltpu.SemaphoreType.DMA((len(parts), CHUNKS + 1)),
            ],
        ),
        out_shape=[jax.ShapeDtypeStruct((1, part + TAG_ROWS, width), jnp.bfloat16) for part in parts],
        compiler_params=pltpu.CompilerParams(vmem_limit_bytes=60 << 20),
        cost_estimate=SMALL_COST,
    )(lengths, embeddings, *earlier)


def pass_kernel(*refs):
    del refs


def after(value, *earlier):
    spec = pl.BlockSpec(memory_space=pl.ANY)
    return pl.pallas_call(
        pass_kernel,
        in_specs=[spec] * (1 + len(earlier)),
        out_specs=spec,
        out_shape=jax.ShapeDtypeStruct(value.shape, value.dtype),
        input_output_aliases={0: 0},
        cost_estimate=SMALL_COST,
    )(value, *earlier)


def match_kernel(meta, *refs, lefts, rights, offset):
    refs = list(refs)
    left_refs = [[refs.pop(0) for _ in range(parts)] for parts in lefts]
    right_refs = [[refs.pop(0) for _ in range(parts)] for parts in rights]
    (peak_in, sum_in, row_ref, peak_ref, sum_ref, left_buf, tags, right_buf, scores, peak, total, items, waiting,
     left_sem, tag_sem, right_sem) = refs
    lefts = len(lefts)
    rights = len(rights)
    row_tile = scores.shape[0]
    left_rows = left_buf.shape[1]
    right_rows = peak_ref.shape[2]
    col_tile = min(COL_TILE, right_rows)
    most = (meta.shape[0] - 1) // 2
    pairs = meta[0]

    def copies(parts, buf, sems):
        made = []
        start = 0
        for n, part in enumerate(parts):
            rows = part.shape[1] - TAG_ROWS
            to = buf.at[pl.ds(start, rows), :]
            made.append(pltpu.make_async_copy(part.at[0, pl.ds(0, rows), :], to, sems.at[n]))
            start += rows
        return made

    def left_copies(k):
        return copies(left_refs[k], left_buf.at[k], left_sem.at[k])

    def right_copies(k):
        return copies(right_refs[k], right_buf.at[k], right_sem.at[k])

    def tag_copy(k):
        part = (left_refs + right_refs)[k][0]
        tag_at = pl.ds(part.shape[1] - TAG_ROWS, TAG_ROWS)
        return pltpu.make_async_copy(part.at[0, tag_at, :], tags.at[k], tag_sem.at[k])

    def start(made):
        for copy in made:
            copy.start()

    def wait(made):
        for copy in made:
            copy.wait()

    for k in range(lefts + rights):
        tag_copy(k).start()

    def fetch(p):
        for k in range(rights):

            @pl.when((p < pairs) & (meta[1 + most + jnp.minimum(p, most - 1)] == k))
            def _():
                start(right_copies(k))

    start(left_copies(0))
    fetch(0)
    for k in range(1, lefts):
        start(left_copies(k))
    waiting[0] = 0

    row_ref[...] = jnp.zeros_like(row_ref)
    peak_ref[...] = peak_in[...]
    sum_ref[...] = sum_in[...]
    for k in range(lefts + rights):
        tag_copy(k).wait()
    left_lens = [jnp.clip(length_of(tags[k]) - offset, 0, left_rows) for k in range(lefts)]
    right_lens = [length_of(tags[lefts + k]) for k in range(rights)]

    def pick(values, index):
        found = values[0]
        for k in range(1, len(values)):
            found = jnp.where(index == k, values[k], found)
        return found

    def list_pair(p, n):
        left = meta[1 + p]
        right = meta[1 + most + p]
        left_len = pick(left_lens, left)
        right_len = pick(right_lens, right)

        def list_block(i, n):
            items[0, n] = left
            items[1, n] = right
            items[2, n] = i
            items[3, n] = left_len - i * row_tile
            items[4, n] = right_len
            items[5, n] = p
            return n + 1

        return lax.fori_loop(0, lax.div(left_len + row_tile - 1, row_tile), list_block, n)

    count = lax.fori_loop(0, pairs, list_pair, 0)
    for k in range(lefts):
        wait(left_copies(k))

    def at(index, size):
        return pl.ds(pl.multiple_of(index * size, size), size)

    def block(item, width):
        left = items[0, item]
        right = items[1, item]
        rows = at(items[2, item], row_tile)
        col_at = lax.broadcasted_iota(jnp.int32, (1, width), 1)
        col_bias = jnp.where(col_at < items[4, item], 0.0, LOWEST)
        row_at = lax.broadcasted_iota(jnp.int32, (row_tile, 1), 0)
        row_bias = jnp.where(row_at < items[3, item], 0.0, LOWEST)
        tile = lax.dot_general(
            left_buf[left, rows, :], right_buf[right, 0:width, :], (((1,), (1,)), ((), ())),
            preferred_element_type=jnp.float32,
        )
        tile = (tile * SCALE + col_bias) + row_bias
        scores[:, 0:width] = tile
        row_peak = tile[:, 0:LANES]
        for k in range(LANES, width, LANES):
            row_peak = jnp.maximum(row_peak, tile[:, k : k + LANES])
        peak[...] = row_peak
        old = peak_ref[right, :, 0:width]
        new = jnp.maximum(old, jnp.max(tile, axis=0, keepdims=True))
        peak_ref[right, :, 0:width] = new
        col_sum = jnp.zeros((8, width), jnp.float32)
        for start in range(0, row_tile, SUM_STEP):
            part = scores[start : start + SUM_STEP, 0:width]
            part_peak = peak[start : start + SUM_STEP, :]
            row_sum = jnp.exp2(part[:, 0:LANES] - part_peak)
            for k in range(LANES, width, LANES):
                row_sum = row_sum + jnp.exp2(part[:, k : k + LANES] - part_peak)
            total[start : start + SUM_STEP, :] = row_sum
            terms = jnp.exp2(part - new)
            col_sum = col_sum + jnp.sum(terms.reshape(SUM_STEP // 8, 8, width), axis=0)
        before = sum_ref[right, :, 0:width]
        sum_ref[right, :, 0:width] = before * jnp.exp2(old - new) + jnp.sum(col_sum, axis=0, keepdims=True)
        lane_peak = jnp.transpose(peak[...])
        lane_sum = jnp.transpose(total[...])
        top = jnp.max(lane_peak, axis=0, keepdims=True)
        all_sum = jnp.sum(lane_sum * jnp.exp2(lane_peak - top), axis=0, keepdims=True)
        row_ref[left, :, rows] = row_ref[left, :, rows] + (top + jnp.log2(all_sum)) * (1.0 / SCALE)

    def ready(item):
        pair = items[5, item]

        @pl.when(waiting[0] <= pair)
        def _():
            fetch(pair + 1)
            right = items[1, item]
            for k in range(rights):

                @pl.when(right == k)
                def _():
                    wait(right_copies(k))

            waiting[0] = pair + 1

    @pl.when(count == 0)
    def _():
        for k in range(rights):

            @pl.when(meta[1 + most] == k)
            def _():
                wait(right_copies(k))

    def one(item, carry):
        ready(item)
        tiles = lax.div(items[4, item] + col_tile - 1, col_tile)
        for n in range(1, right_rows // col_tile + 1):

            @pl.when(tiles == n)
            def _():
                block(item, n * col_tile)

        return carry

    lax.fori_loop(0, count, one, 0)


def match(meta, lefts, rights, offset=0, carried=None):
    count = len(rights)
    width = rights[0][0].shape[2]
    left_rows = sum(part.shape[1] - TAG_ROWS for part in lefts[0])
    right_rows = sum(part.shape[1] - TAG_ROWS for part in rights[0])
    row_tile = min(ROW_TILE, left_rows)
    most = (meta.shape[0] - 1) // 2
    blocks = most * (left_rows // row_tile)
    left_parts = [len(parts) for parts in lefts]
    right_parts = [len(parts) for parts in rights]
    packets = [part for parts in lefts + rights for part in parts]
    if carried is None:
        carried = (
            jnp.full((count, 1, right_rows), LOWEST, jnp.float32),
            jnp.zeros((count, 1, right_rows), jnp.float32),
        )
    anywhere = pl.BlockSpec(memory_space=pl.ANY)
    row_shape = (len(lefts), 1, left_rows)
    col_shape = (count, 1, right_rows)
    row_spec = pl.BlockSpec(row_shape, lambda p, m: (0, 0, 0))
    col_spec = pl.BlockSpec(col_shape, lambda p, m: (0, 0, 0))
    rows, peaks, sums = pl.pallas_call(
        functools.partial(match_kernel, lefts=left_parts, rights=right_parts, offset=offset),
        grid_spec=pltpu.PrefetchScalarGridSpec(
            num_scalar_prefetch=1,
            grid=(1,),
            in_specs=[anywhere] * len(packets) + [col_spec, col_spec],
            out_specs=[row_spec, col_spec, col_spec],
            scratch_shapes=[
                pltpu.VMEM((len(lefts), left_rows, width), jnp.bfloat16),
                pltpu.VMEM((len(lefts) + count, TAG_ROWS, width), jnp.bfloat16),
                pltpu.VMEM((count, right_rows, width), jnp.bfloat16),
                pltpu.VMEM((row_tile, right_rows), jnp.float32),
                pltpu.VMEM((row_tile, LANES), jnp.float32),
                pltpu.VMEM((row_tile, LANES), jnp.float32),
                pltpu.SMEM((6, blocks), jnp.int32),
                pltpu.SMEM((1,), jnp.int32),
                pltpu.SemaphoreType.DMA((len(lefts), max(left_parts))),
                pltpu.SemaphoreType.DMA((len(lefts) + count,)),
                pltpu.SemaphoreType.DMA((count, max(right_parts))),
            ],
        ),
        out_shape=[
            jax.ShapeDtypeStruct(row_shape, jnp.float32),
            jax.ShapeDtypeStruct(col_shape, jnp.float32),
            jax.ShapeDtypeStruct(col_shape, jnp.float32),
        ],
        compiler_params=pltpu.CompilerParams(vmem_limit_bytes=32 << 20),
        cost_estimate=SMALL_COST,
    )(meta, *packets, *carried)
    return rows[:, 0], (peaks, sums)


def matches_of(active, carried):
    peaks, sums = carried
    return jnp.where(active[:, None], (peaks + jnp.log2(sums))[:, 0] * (1.0 / SCALE), 0.0)


def shards(embeddings, lengths):
    answers, length, _ = embeddings.shape
    count = lax.axis_size("cand")
    is_even = lax.axis_index("cand") % 2 == 0

    first_to = [(i, (i - 2 if i % 2 == 0 else i + 2) % count) for i in range(count)]
    second_to = [(i, (i - 1 if i % 2 == 0 else i + 1) % count) for i in range(count)]
    mate_to = [(i, i ^ 1) for i in range(count)]

    def move(value, pairs):
        return lax.ppermute(value, "cand", pairs)

    def back(value, pairs):
        return lax.ppermute(value, "cand", [(b, a) for a, b in pairs])

    def by_role(even, odd):
        return jnp.where(is_even, jnp.array(even, jnp.int32), jnp.array(odd, jnp.int32))

    half = length // 2
    halves = [half, length - half]
    whole_first, *own_first = packets_of(embeddings, lengths, 0, [length] + halves)
    first = move(whole_first, first_to)
    own_second = packets_of(embeddings, lengths, 1, halves, whole_first)
    mate_first = [move(part, mate_to) for part in own_first]
    mate_second = [move(part, mate_to) for part in own_second]
    near = [own_first, own_second, mate_first, mate_second]
    every = jnp.arange(2 * answers)

    inner_meta = by_role([3, 0, 0, 0, 1, 2, 3], [3, 0, 2, 1, 1, 0, 3])
    inner_rows, inner_cols = match(inner_meta, [own_first, own_second, mate_second], near)

    lower = move(after(own_second[0], inner_rows), second_to)
    upper = move(after(own_second[1], first), second_to)
    first_meta = by_role([4, 0, 0, 0, 0, 0, 1, 2, 3], [2, 0, 0, 0, 0, 0, 1, 1, 1])
    first_rows, first_cols = match(first_meta, [[first]], near)
    first_back = back(first_rows[0], first_to)
    second_meta = by_role([2, 0, 0, 0, 0, 2, 3, 3, 3], [4, 0, 0, 0, 0, 0, 1, 2, 3])
    lower_rows, second_cols = match(second_meta, [[lower]], near)
    upper_rows, second_cols = match(second_meta, [[upper]], near, half, second_cols)
    second_back = back(jnp.concatenate([lower_rows[0], upper_rows[0]]), second_to)

    zero = jnp.zeros_like(inner_rows[0])
    totals = jnp.stack([inner_rows[0], inner_rows[1], zero, inner_rows[2]])
    totals = totals + matches_of(jnp.where(is_even, every > 0, every != 2), inner_cols)
    totals = totals + matches_of(is_even | (every < answers), first_cols)
    totals = totals + matches_of(~is_even | (every >= answers), second_cols)
    mate_back = move(totals[answers:], mate_to)

    consensus = totals[:answers] + mate_back + jnp.stack([first_back, second_back])
    inside = lax.broadcasted_iota(jnp.int32, (answers, length), 1) < lengths[:, None]
    return jnp.where(inside, consensus / (answers - 1 + 4 * answers), 0.0)


def solution(mesh):
    return jax.shard_map(
        shards,
        mesh=mesh,
        in_specs=(P(("group", "cand"), None, None), P(("group", "cand"))),
        out_specs=P(("group", "cand"), None),
        check_vma=False,
    )
```

```python
import functools

import jax
import jax.numpy as jnp
from jax import lax
from jax.experimental import pallas as pl
from jax.experimental.pallas import tpu as pltpu
from jax.sharding import PartitionSpec as P

SCALE = 256.0 * 1.4426950408889634
LOWEST = -1e30
LANES = 128
TAG_ROWS = 16
TAG_BASE = 64
ROW_TILE = 512
COL_TILE = 256
SUM_STEP = 64
CHUNKS = 4
SMALL_COST = pl.CostEstimate(flops=1, bytes_accessed=1, transcendentals=0)


def unit_rows(embeddings):
    values = embeddings.astype(jnp.float32)
    scale = lax.rsqrt(jnp.sum(values * values, axis=-1, keepdims=True) + 1e-06)
    return (values * scale).astype(jnp.bfloat16)


def length_of(tag):
    values = tag.astype(jnp.float32)
    upper = lax.broadcasted_iota(jnp.int32, values.shape, 0) < TAG_ROWS // 2
    high = jnp.max(jnp.where(upper, values, 0.0)).astype(jnp.int32)
    low = jnp.max(jnp.where(upper, 0.0, values)).astype(jnp.int32)
    return high * TAG_BASE + low


def packet_kernel(lengths, values_ref, *refs, slot, rows, outs):
    packet_refs = refs[-outs - 4 : -4]
    values_buf, packet_buf, in_sem, out_sem = refs[-4:]
    chunk = rows // CHUNKS
    tags = pl.ds(rows, TAG_ROWS)
    parts = [packet_ref.shape[1] - TAG_ROWS for packet_ref in packet_refs]
    starts = [sum(parts[:k]) % rows for k in range(outs)]

    def copy_in(k):
        at = pl.ds(k * chunk, chunk)
        return pltpu.make_async_copy(values_ref.at[slot, at, :], values_buf.at[at, :], in_sem.at[k])

    def tag_out(k):
        to = packet_refs[k].at[0, pl.ds(parts[k], TAG_ROWS), :]
        return pltpu.make_async_copy(packet_buf.at[tags, :], to, out_sem.at[k, CHUNKS])

    def copies_out(c):
        copies = []
        for k in range(outs):
            offset = c * chunk - starts[k]
            if 0 <= offset < parts[k]:
                to = packet_refs[k].at[0, pl.ds(offset, chunk), :]
                copies.append(pltpu.make_async_copy(packet_buf.at[pl.ds(c * chunk, chunk), :], to, out_sem.at[k, c]))
        return copies

    for c in range(CHUNKS):
        copy_in(c).start()
    shape = (TAG_ROWS, values_buf.shape[1])
    upper = lax.broadcasted_iota(jnp.int32, shape, 0) < TAG_ROWS // 2
    tag = jnp.where(upper, lengths[slot] // TAG_BASE, lengths[slot] % TAG_BASE)
    packet_buf[tags, :] = tag.astype(jnp.float32).astype(jnp.bfloat16)
    for k in range(outs):
        tag_out(k).start()
    for c in range(CHUNKS):
        copy_in(c).wait()
        at = pl.ds(c * chunk, chunk)
        packet_buf[at, :] = unit_rows(values_buf[at, :])
        for copy in copies_out(c):
            copy.start()
    for c in range(CHUNKS):
        for copy in copies_out(c):
            copy.wait()
    for k in range(outs):
        tag_out(k).wait()


def packets_of(embeddings, lengths, slot, parts, *earlier):
    _, rows, width = embeddings.shape
    anywhere = pl.BlockSpec(memory_space=pl.ANY)
    return pl.pallas_call(
        functools.partial(packet_kernel, slot=slot, rows=rows, outs=len(parts)),
        grid_spec=pltpu.PrefetchScalarGridSpec(
            num_scalar_prefetch=1,
            grid=(1,),
            in_specs=[anywhere] * (1 + len(earlier)),
            out_specs=[anywhere] * len(parts),
            scratch_shapes=[
                pltpu.VMEM((rows, width), jnp.bfloat16),
                pltpu.VMEM((rows + TAG_ROWS, width), jnp.bfloat16),
                pltpu.SemaphoreType.DMA((CHUNKS,)),
                pltpu.SemaphoreType.DMA((len(parts), CHUNKS + 1)),
            ],
        ),
        out_shape=[jax.ShapeDtypeStruct((1, part + TAG_ROWS, width), jnp.bfloat16) for part in parts],
        compiler_params=pltpu.CompilerParams(vmem_limit_bytes=60 << 20),
        cost_estimate=SMALL_COST,
    )(lengths, embeddings, *earlier)


def pass_kernel(*refs):
    del refs


def after(value, *earlier):
    spec = pl.BlockSpec(memory_space=pl.ANY)
    return pl.pallas_call(
        pass_kernel,
        in_specs=[spec] * (1 + len(earlier)),
        out_specs=spec,
        out_shape=jax.ShapeDtypeStruct(value.shape, value.dtype),
        input_output_aliases={0: 0},
        cost_estimate=SMALL_COST,
    )(value, *earlier)


def match_kernel(meta, *refs, lefts, rights, offset):
    refs = list(refs)
    left_refs = [[refs.pop(0) for _ in range(parts)] for parts in lefts]
    right_refs = [[refs.pop(0) for _ in range(parts)] for parts in rights]
    (peak_in, sum_in, row_ref, peak_ref, sum_ref, left_buf, tags, right_buf, scores, peak, total, items, waiting,
     left_sem, tag_sem, right_sem) = refs
    lefts = len(lefts)
    rights = len(rights)
    row_tile = scores.shape[0]
    left_rows = left_buf.shape[1]
    right_rows = peak_ref.shape[2]
    col_tile = min(COL_TILE, right_rows)
    most = (meta.shape[0] - 1) // 2
    pairs = meta[0]

    def copies(parts, buf, sems):
        made = []
        start = 0
        for n, part in enumerate(parts):
            rows = part.shape[1] - TAG_ROWS
            to = buf.at[pl.ds(start, rows), :]
            made.append(pltpu.make_async_copy(part.at[0, pl.ds(0, rows), :], to, sems.at[n]))
            start += rows
        return made

    def left_copies(k):
        return copies(left_refs[k], left_buf.at[k], left_sem.at[k])

    def right_copies(k):
        return copies(right_refs[k], right_buf.at[k], right_sem.at[k])

    def tag_copy(k):
        part = (left_refs + right_refs)[k][0]
        tag_at = pl.ds(part.shape[1] - TAG_ROWS, TAG_ROWS)
        return pltpu.make_async_copy(part.at[0, tag_at, :], tags.at[k], tag_sem.at[k])

    def start(made):
        for copy in made:
            copy.start()

    def wait(made):
        for copy in made:
            copy.wait()

    for k in range(lefts + rights):
        tag_copy(k).start()

    def fetch(p):
        for k in range(rights):

            @pl.when((p < pairs) & (meta[1 + most + jnp.minimum(p, most - 1)] == k))
            def _():
                start(right_copies(k))

    start(left_copies(0))
    fetch(0)
    for k in range(1, lefts):
        start(left_copies(k))
    waiting[0] = 0

    row_ref[...] = jnp.zeros_like(row_ref)
    peak_ref[...] = peak_in[...]
    sum_ref[...] = sum_in[...]
    for k in range(lefts + rights):
        tag_copy(k).wait()
    left_lens = [jnp.clip(length_of(tags[k]) - offset, 0, left_rows) for k in range(lefts)]
    right_lens = [length_of(tags[lefts + k]) for k in range(rights)]

    def pick(values, index):
        found = values[0]
        for k in range(1, len(values)):
            found = jnp.where(index == k, values[k], found)
        return found

    def list_pair(p, n):
        left = meta[1 + p]
        right = meta[1 + most + p]
        left_len = pick(left_lens, left)
        right_len = pick(right_lens, right)

        def list_block(i, n):
            items[0, n] = left
            items[1, n] = right
            items[2, n] = i
            items[3, n] = left_len - i * row_tile
            items[4, n] = right_len
            items[5, n] = p
            return n + 1

        return lax.fori_loop(0, lax.div(left_len + row_tile - 1, row_tile), list_block, n)

    count = lax.fori_loop(0, pairs, list_pair, 0)
    for k in range(lefts):
        wait(left_copies(k))

    def at(index, size):
        return pl.ds(pl.multiple_of(index * size, size), size)

    def block(item, width):
        left = items[0, item]
        right = items[1, item]
        rows = at(items[2, item], row_tile)
        col_at = lax.broadcasted_iota(jnp.int32, (1, width), 1)
        col_bias = jnp.where(col_at < items[4, item], 0.0, LOWEST)
        row_at = lax.broadcasted_iota(jnp.int32, (row_tile, 1), 0)
        row_bias = jnp.where(row_at < items[3, item], 0.0, LOWEST)
        tile = lax.dot_general(
            left_buf[left, rows, :], right_buf[right, 0:width, :], (((1,), (1,)), ((), ())),
            preferred_element_type=jnp.float32,
        )
        tile = (tile * SCALE + col_bias) + row_bias
        scores[:, 0:width] = tile
        row_peak = tile[:, 0:LANES]
        for k in range(LANES, width, LANES):
            row_peak = jnp.maximum(row_peak, tile[:, k : k + LANES])
        peak[...] = row_peak
        old = peak_ref[right, :, 0:width]
        new = jnp.maximum(old, jnp.max(tile, axis=0, keepdims=True))
        peak_ref[right, :, 0:width] = new
        col_sum = jnp.zeros((8, width), jnp.float32)
        for start in range(0, row_tile, SUM_STEP):
            part = scores[start : start + SUM_STEP, 0:width]
            part_peak = peak[start : start + SUM_STEP, :]
            row_sum = jnp.exp2(part[:, 0:LANES] - part_peak)
            for k in range(LANES, width, LANES):
                row_sum = row_sum + jnp.exp2(part[:, k : k + LANES] - part_peak)
            total[start : start + SUM_STEP, :] = row_sum
            terms = jnp.exp2(part - new)
            col_sum = col_sum + jnp.sum(terms.reshape(SUM_STEP // 8, 8, width), axis=0)
        before = sum_ref[right, :, 0:width]
        sum_ref[right, :, 0:width] = before * jnp.exp2(old - new) + jnp.sum(col_sum, axis=0, keepdims=True)
        lane_peak = jnp.transpose(peak[...])
        lane_sum = jnp.transpose(total[...])
        top = jnp.max(lane_peak, axis=0, keepdims=True)
        all_sum = jnp.sum(lane_sum * jnp.exp2(lane_peak - top), axis=0, keepdims=True)
        row_ref[left, :, rows] = row_ref[left, :, rows] + (top + jnp.log2(all_sum)) * (1.0 / SCALE)

    def ready(item):
        pair = items[5, item]

        @pl.when(waiting[0] <= pair)
        def _():
            fetch(pair + 1)
            right = items[1, item]
            for k in range(rights):

                @pl.when(right == k)
                def _():
                    wait(right_copies(k))

            waiting[0] = pair + 1

    @pl.when(count == 0)
    def _():
        for k in range(rights):

            @pl.when(meta[1 + most] == k)
            def _():
                wait(right_copies(k))

    def one(item, carry):
        ready(item)
        tiles = lax.div(items[4, item] + col_tile - 1, col_tile)
        for n in range(1, right_rows // col_tile + 1):

            @pl.when(tiles == n)
            def _():
                block(item, n * col_tile)

        return carry

    lax.fori_loop(0, count, one, 0)


def match(meta, lefts, rights, offset=0, carried=None):
    count = len(rights)
    width = rights[0][0].shape[2]
    left_rows = sum(part.shape[1] - TAG_ROWS for part in lefts[0])
    right_rows = sum(part.shape[1] - TAG_ROWS for part in rights[0])
    row_tile = min(ROW_TILE, left_rows)
    most = (meta.shape[0] - 1) // 2
    blocks = most * (left_rows // row_tile)
    left_parts = [len(parts) for parts in lefts]
    right_parts = [len(parts) for parts in rights]
    packets = [part for parts in lefts + rights for part in parts]
    if carried is None:
        carried = (
            jnp.full((count, 1, right_rows), LOWEST, jnp.float32),
            jnp.zeros((count, 1, right_rows), jnp.float32),
        )
    anywhere = pl.BlockSpec(memory_space=pl.ANY)
    row_shape = (len(lefts), 1, left_rows)
    col_shape = (count, 1, right_rows)
    row_spec = pl.BlockSpec(row_shape, lambda p, m: (0, 0, 0))
    col_spec = pl.BlockSpec(col_shape, lambda p, m: (0, 0, 0))
    rows, peaks, sums = pl.pallas_call(
        functools.partial(match_kernel, lefts=left_parts, rights=right_parts, offset=offset),
        grid_spec=pltpu.PrefetchScalarGridSpec(
            num_scalar_prefetch=1,
            grid=(1,),
            in_specs=[anywhere] * len(packets) + [col_spec, col_spec],
            out_specs=[row_spec, col_spec, col_spec],
            scratch_shapes=[
                pltpu.VMEM((len(lefts), left_rows, width), jnp.bfloat16),
                pltpu.VMEM((len(lefts) + count, TAG_ROWS, width), jnp.bfloat16),
                pltpu.VMEM((count, right_rows, width), jnp.bfloat16),
                pltpu.VMEM((row_tile, right_rows), jnp.float32),
                pltpu.VMEM((row_tile, LANES), jnp.float32),
                pltpu.VMEM((row_tile, LANES), jnp.float32),
                pltpu.SMEM((6, blocks), jnp.int32),
                pltpu.SMEM((1,), jnp.int32),
                pltpu.SemaphoreType.DMA((len(lefts), max(left_parts))),
                pltpu.SemaphoreType.DMA((len(lefts) + count,)),
                pltpu.SemaphoreType.DMA((count, max(right_parts))),
            ],
        ),
        out_shape=[
            jax.ShapeDtypeStruct(row_shape, jnp.float32),
            jax.ShapeDtypeStruct(col_shape, jnp.float32),
            jax.ShapeDtypeStruct(col_shape, jnp.float32),
        ],
        compiler_params=pltpu.CompilerParams(vmem_limit_bytes=32 << 20),
        cost_estimate=SMALL_COST,
    )(meta, *packets, *carried)
    return rows[:, 0], (peaks, sums)


def matches_of(active, carried):
    peaks, sums = carried
    return jnp.where(active[:, None], (peaks + jnp.log2(sums))[:, 0] * (1.0 / SCALE), 0.0)


def shards(embeddings, lengths):
    answers, length, _ = embeddings.shape
    count = lax.axis_size("cand")
    is_even = lax.axis_index("cand") % 2 == 0

    first_to = [(i, (i - 2 if i % 2 == 0 else i + 2) % count) for i in range(count)]
    second_to = [(i, (i - 1 if i % 2 == 0 else i + 1) % count) for i in range(count)]
    mate_to = [(i, i ^ 1) for i in range(count)]

    def move(value, pairs):
        return lax.ppermute(value, "cand", pairs)

    def back(value, pairs):
        return lax.ppermute(value, "cand", [(b, a) for a, b in pairs])

    def by_role(even, odd):
        return jnp.where(is_even, jnp.array(even, jnp.int32), jnp.array(odd, jnp.int32))

    half = length // 2
    halves = [half, length - half]
    whole_first, *own_first = packets_of(embeddings, lengths, 0, [length] + halves)
    first = move(whole_first, first_to)
    own_second = packets_of(embeddings, lengths, 1, halves, whole_first)
    mate_first = [move(part, mate_to) for part in own_first]
    mate_second = [move(part, mate_to) for part in own_second]
    near = [own_first, own_second, mate_first, mate_second]
    every = jnp.arange(2 * answers)

    inner_meta = by_role([3, 0, 0, 0, 1, 2, 3], [3, 0, 2, 1, 1, 0, 3])
    inner_rows, inner_cols = match(inner_meta, [own_first, own_second, mate_second], near)

    lower = move(after(own_second[0], inner_rows), second_to)
    upper = move(after(own_second[1], first, lower), second_to)
    first_meta = by_role([4, 0, 0, 0, 0, 0, 1, 2, 3], [2, 0, 0, 0, 0, 0, 1, 1, 1])
    first_rows, first_cols = match(first_meta, [[first]], near)
    first_back = back(first_rows[0], first_to)
    second_meta = by_role([2, 0, 0, 0, 0, 2, 3, 3, 3], [4, 0, 0, 0, 0, 0, 1, 2, 3])
    lower_rows, second_cols = match(second_meta, [[lower]], near)
    upper_rows, second_cols = match(second_meta, [[upper]], near, half, second_cols)
    second_back = back(jnp.concatenate([lower_rows[0], upper_rows[0]]), second_to)

    zero = jnp.zeros_like(inner_rows[0])
    totals = jnp.stack([inner_rows[0], inner_rows[1], zero, inner_rows[2]])
    totals = totals + matches_of(jnp.where(is_even, every > 0, every != 2), inner_cols)
    totals = totals + matches_of(is_even | (every < answers), first_cols)
    totals = totals + matches_of(~is_even | (every >= answers), second_cols)
    mate_back = move(totals[answers:], mate_to)

    consensus = totals[:answers] + mate_back + jnp.stack([first_back, second_back])
    inside = lax.broadcasted_iota(jnp.int32, (answers, length), 1) < lengths[:, None]
    return jnp.where(inside, consensus / (answers - 1 + 4 * answers), 0.0)


def solution(mesh):
    return jax.shard_map(
        shards,
        mesh=mesh,
        in_specs=(P(("group", "cand"), None, None), P(("group", "cand"))),
        out_specs=P(("group", "cand"), None),
        check_vma=False,
    )
```
